32 devices in a mesh: groups: 1, freq: 32 (over z, y, x, core).
Axes of the slice: x: 2, y: 2, z: 4, core: 2. Of those that a mesh axis runs over, the one named last changes fastest.
Arguments:
- mag_field: float32 [2, 256, 16384], P(None, 'groups', 'freq'), may hold values from -6 to 6
- node_order: int32 [256], P('groups'), may hold values from 0 to 255, each once
- source_blocks: int32 [4, 4], P('groups'), may hold values from 0 to 3
- impedance: float32 [4, 8, 4, 8192], P(None, None, 'groups', 'freq'), may hold values from -4 to 4
Outputs:
- electric_field: float32 [2, 256, 16384], P(None, 'groups', 'freq')
The draws below stay inside these ranges and needn't reach their ends.
Inputs may be any that keep to these rules, and one draw needn't show every extreme that they name: node_order holds every node exactly once. `source_blocks`: block numbers; a block may be listed more than once.
All inputs are finite; a program needn't handle non-finite values.
Results may differ from the reference program's by a relative error of at most 0.00007.
Values sent between devices are 32-bit elements; how exact they have to be, the bound alone decides.
A program may use at most 64 MiB of HBM per device.

```python
import jax
import jax.numpy as jnp
from jax import lax

NT = 16384
HALF_SPECTRUM = 8192
NODES = 256
BSIZE = 64
BLOCKS = 4
NBR = 4


def place_ends(array, stream_key, smallest, largest):
    spot = [jax.random.randint(jax.random.fold_in(stream_key, axis), (), 0, length) for axis, length in enumerate(array.shape)]
    main_axis = array.shape.index(max(array.shape))
    next_to = spot[:main_axis] + [(spot[main_axis] + 1) % array.shape[main_axis]] + spot[main_axis + 1:]
    return array.at[tuple(spot)].set(smallest).at[tuple(next_to)].set(largest)


def level_of(own_key, dims, pieces, low, largest):
    def one(axis_at, blocks):
        heights = jax.random.uniform(jax.random.fold_in(jax.random.fold_in(own_key, 6), axis_at), (blocks,), jnp.float32, low / len(pieces), largest / len(pieces))
        return jnp.repeat(jnp.exp(heights), dims[axis_at] // blocks).reshape((-1,) + (1,) * (len(dims) - axis_at - 1))

    factor_of = one(*pieces[0])
    for cut in pieces[1:]:
        factor_of = factor_of * one(*cut)
    return factor_of


def normal_values(key, extent, deviation, reach, split=(), held_as=jnp.bfloat16):
    values = deviation * jax.random.normal(key, extent, jnp.float32)
    if split:
        values = values * level_of(key, extent, split, -0.22, 0.18)
    return jnp.clip(values, -reach, reach).astype(held_as)


def setup_inputs(seed: int = 0, part: int = 0) -> dict:
    streams_of = jax.random.split(jax.random.key(seed), 5)
    own_keys = jax.random.split(jax.random.fold_in(streams_of[4], part), 5)
    return {
        "mag_field": normal_values(own_keys[0], (2, NODES, NT), 1.0, 6.0, ((2, 32),), jnp.float32),
        "node_order": jax.random.permutation(own_keys[1], NODES).astype(jnp.int32),
        "source_blocks": place_ends(jax.random.randint(own_keys[2], (BLOCKS, NBR), 0, BLOCKS), jax.random.fold_in(own_keys[2], 1), 0, BLOCKS - 1).astype(jnp.int32),
        "impedance": normal_values(own_keys[3], (NBR, 8, BLOCKS, HALF_SPECTRUM), 0.5, 4.0, ((3, 32),), jnp.float32),
    }


def reference(mag_field, node_order, source_blocks, impedance):
    spectrum = jnp.fft.fft(lax.complex(mag_field[0], mag_field[1]), axis=-1)
    positive = spectrum[:, :HALF_SPECTRUM]
    mirrored = jnp.concatenate([spectrum[:, :1], spectrum[:, :HALF_SPECTRUM:-1]], axis=1)
    bx_hat = (positive + jnp.conj(mirrored)) * 0.5
    by_hat = (positive - jnp.conj(mirrored)) * (-0.5j)
    slots = node_order.reshape(BLOCKS, BSIZE)
    tensors = lax.complex(impedance[:, 0::2], impedance[:, 1::2])
    ex_block = jnp.zeros((BLOCKS, BSIZE, HALF_SPECTRUM), spectrum.dtype)
    ey_block = jnp.zeros((BLOCKS, BSIZE, HALF_SPECTRUM), spectrum.dtype)
    for source in range(NBR):
        nodes_src = slots[source_blocks[:, source]]
        bx_src = bx_hat[nodes_src]
        by_src = by_hat[nodes_src]
        ex_block = ex_block + tensors[source, 0][:, None, :] * bx_src + tensors[source, 1][:, None, :] * by_src
        ey_block = ey_block + tensors[source, 2][:, None, :] * bx_src + tensors[source, 3][:, None, :] * by_src
    keep = (jnp.arange(HALF_SPECTRUM) > 0)[None, None, :]
    ex_block = jnp.where(keep, ex_block, jnp.zeros_like(ex_block))
    ey_block = jnp.where(keep, ey_block, jnp.zeros_like(ey_block))
    east_field_nodes = jnp.zeros((NODES, HALF_SPECTRUM), spectrum.dtype).at[node_order].set(ex_block.reshape(NODES, HALF_SPECTRUM))
    north_field_nodes = jnp.zeros((NODES, HALF_SPECTRUM), spectrum.dtype).at[node_order].set(ey_block.reshape(NODES, HALF_SPECTRUM))
    packed_upper = east_field_nodes + 1j * north_field_nodes
    packed_reflected = jnp.conj(east_field_nodes) + 1j * jnp.conj(north_field_nodes)
    packed_spectrum = jnp.concatenate([packed_upper, jnp.zeros_like(packed_upper[:, :1]), packed_reflected[:, :0:-1]], axis=1)
    series = jnp.fft.ifft(packed_spectrum, axis=-1)
    return jnp.stack([jnp.real(series), jnp.imag(series)])
```

```python
import functools
import math

import jax
import jax.numpy as jnp
import ml_dtypes
import numpy as np
from jax import lax
from jax.experimental import pallas as pl
from jax.experimental.pallas import tpu as pltpu
from jax.sharding import PartitionSpec as P

NT = 16384
HALF_SPECTRUM = 8192
BSIZE = 64
NBR = 4
LANES = 128
VMEM_LIMIT = 48 * 1024 * 1024


def split_bf16(table):
    high = table.astype(ml_dtypes.bfloat16)
    low = (table - high.astype(np.float64)).astype(ml_dtypes.bfloat16)
    return high, low


def build_tables(devices):
    span = NT // devices
    groups = LANES // devices
    lane = np.arange(span // 2)
    kappa = (lane % 64) * groups + lane // 64
    theta = 2.0 * math.pi / span * (np.arange(span)[:, None] * kappa[None, :] % span)
    cosine, sine = np.cos(theta), np.sin(theta)
    forward = np.block([[cosine, -sine], [sine, cosine]])
    inverse = np.block([[cosine.T, sine.T], [-sine.T, cosine.T]]) * (2.0 / NT)
    phi = 2.0 * math.pi / NT * (np.arange(devices)[:, None] * np.arange(span)[None, :])
    twist = np.stack([np.cos(phi), np.sin(phi)]).astype(np.float32)
    return split_bf16(forward), split_bf16(inverse), twist


def times(a, b):
    return a * b if abs(abs(b) - 1.0) > 1e-12 else (a if b > 0 else -a)


def rotate(re, im, angle):
    c, s = math.cos(angle), math.sin(angle)
    if abs(c - abs(s)) < 1e-12:
        return ((re - im) * c, (re + im) * c) if s > 0 else ((re + im) * c, (im - re) * c)
    return re * c - im * s, re * s + im * c


def real_dft(x):
    n = len(x)
    if n == 2:
        return [(x[0] + x[1], None), (x[0] - x[1], None)]
    even, odd = real_dft(x[0::2]), real_dft(x[1::2])
    out = [None] * (n // 2 + 1)
    out[0] = (even[0][0] + odd[0][0], None)
    out[n // 2] = (even[0][0] - odd[0][0], None)
    out[n // 4] = (even[n // 4][0], -odd[n // 4][0])
    for k in range(1, n // 4):
        tr, ti = rotate(odd[k][0], odd[k][1], -2.0 * math.pi * k / n)
        er, ei = even[k]
        out[k] = (er + tr, ei + ti)
        out[n // 2 - k] = (er - tr, ti - ei)
    return out


def real_idft(spec):
    n = 2 * (len(spec) - 1)
    if n == 2:
        return [spec[0][0] + spec[1][0], spec[0][0] - spec[1][0]]
    even = [(spec[0][0] + spec[n // 2][0], None)]
    odd = [(spec[0][0] - spec[n // 2][0], None)]
    for k in range(1, n // 4):
        ar, ai = spec[k]
        br, bi = spec[n // 2 - k]
        even.append((ar + br, ai - bi))
        odd.append(rotate(ar - br, ai + bi, 2.0 * math.pi * k / n))
    mr, mi = spec[n // 4]
    even.append((mr + mr, None))
    odd.append((-(mi + mi), None))
    out = [None] * n
    out[0::2] = real_idft(even)
    out[1::2] = real_idft(odd)
    return out


def matmul3(high, low, w_high, w_low):
    dot = functools.partial(jnp.dot, preferred_element_type=jnp.float32)
    return dot(high, w_high) + (dot(low, w_high) + dot(high, w_low))


def store_split(high_ref, low_ref, index, value):
    high = value.astype(jnp.bfloat16)
    high_ref[index] = high
    low_ref[index] = (value - high.astype(jnp.float32)).astype(jnp.bfloat16)


def forward_slot(read, y_ref, zh_ref, zl_ref, wh_ref, wl_ref, tw_ref, b_ref, devices, fields):
    span = NT // devices
    half = devices // 2
    for c in range(span // LANES):
        spec = real_dft([read(t, c) for t in range(devices)])
        for p in range(devices):
            re, im = spec[p] if p <= half else spec[devices - p]
            im = jnp.zeros_like(re) if im is None else (im if p <= half else -im)
            y_ref[0, c, pl.ds(p, fields, stride=devices), :] = re
            y_ref[1, c, pl.ds(p, fields, stride=devices), :] = im
    for c in range(span // LANES):
        lanes = slice(c * LANES, (c + 1) * LANES)
        tc, ts = tw_ref[0, :, lanes], tw_ref[1, :, lanes]
        for f in range(fields):
            rows = slice(f * devices, (f + 1) * devices)
            yr, yi = y_ref[0, c, rows, :], y_ref[1, c, rows, :]
            store_split(zh_ref, zl_ref, (rows, lanes), yr * tc + yi * ts)
            imag_lanes = slice(span + c * LANES, span + (c + 1) * LANES)
            store_split(zh_ref, zl_ref, (rows, imag_lanes), yi * tc - yr * ts)
    b_ref[...] = matmul3(zh_ref[...], zl_ref[...], wh_ref[...], wl_ref[...])


def turn_impedance(zg_ref, zt_ref, devices, count):
    groups = LANES // devices
    lane = lax.broadcasted_iota(jnp.int32, (devices, LANES), 1)
    row = lax.broadcasted_iota(jnp.int32, (devices, LANES), 0)
    left = lane < 64
    keep = (lane + row) > 0

    def step(i, carry):
        a = 2 * i
        pair = jnp.concatenate(
            [zg_ref[pl.ds(a, 64, stride=count), :], zg_ref[pl.ds(a + 1, 64, stride=count), :]], axis=0
        ).T
        for g in range(0, groups, 2):
            s0 = pair[g * devices : (g + 1) * devices, :]
            s1 = pair[(g + 1) * devices : (g + 2) * devices, :]
            first = jnp.where(left, s0, pltpu.roll(s1, 64, 1))
            second = jnp.where(left, pltpu.roll(s0, 64, 1), s1)
            if g == 0:
                first = jnp.where(keep, first, 0.0)
                second = jnp.where(keep, second, 0.0)
            lanes = slice(g * 64, g * 64 + LANES)
            zt_ref[a, :, lanes] = first
            zt_ref[a + 1, :, lanes] = second
        return carry

    lax.fori_loop(0, count // 2, step, 0)


def mix_slot(b_ref, zt_ref, sb_ref, eh_ref, el_ref, devices, blocks):
    kap = NT // devices // 2
    tile = 16

    def block_step(b, carry):
        for pt in range(devices // tile):
            for lt in range(kap // LANES):
                lanes = slice(lt * LANES, (lt + 1) * LANES)
                ilanes = slice(kap + lt * LANES, kap + (lt + 1) * LANES)
                acc = [None] * 4
                for r in range(NBR):
                    src = sb_ref[b, r]
                    xrow = pl.ds(pl.multiple_of(src * devices + pt * tile, tile), tile)
                    yrow = pl.ds(pl.multiple_of((blocks + src) * devices + pt * tile, tile), tile)
                    bxr, bxi = b_ref[xrow, lanes], b_ref[xrow, ilanes]
                    byr, byi = b_ref[yrow, lanes], b_ref[yrow, ilanes]
                    z = [
                        zt_ref[(r * 8 + q) * blocks + b, pt * tile : (pt + 1) * tile, lanes]
                        for q in range(8)
                    ]
                    terms = [
                        z[0] * bxr - z[1] * bxi + z[2] * byr - z[3] * byi,
                        z[0] * bxi + z[1] * bxr + z[2] * byi + z[3] * byr,
                        z[4] * bxr - z[5] * bxi + z[6] * byr - z[7] * byi,
                        z[4] * bxi + z[5] * bxr + z[6] * byi + z[7] * byr,
                    ]
                    acc = [t if a is None else a + t for a, t in zip(acc, terms)]
                for comp in range(2):
                    rows = pl.ds(pl.multiple_of((comp * blocks + b) * devices + pt * tile, tile), tile)
                    store_split(eh_ref, el_ref, (rows, lanes), acc[2 * comp])
                    store_split(eh_ref, el_ref, (rows, ilanes), acc[2 * comp + 1])
        return carry

    lax.fori_loop(0, blocks, block_step, 0)


def inverse_slot(eh_ref, el_ref, g_ref, y_ref, wh_ref, wl_ref, tw_ref, write, devices, fields):
    span = NT // devices
    half = devices // 2
    g_ref[...] = matmul3(eh_ref[...], el_ref[...], wh_ref[...], wl_ref[...])
    for c in range(span // LANES):
        lanes = slice(c * LANES, (c + 1) * LANES)
        ilanes = slice(span + c * LANES, span + (c + 1) * LANES)
        tc, ts = tw_ref[0, :, lanes], tw_ref[1, :, lanes]
        for f in range(fields):
            rows = slice(f * devices, (f + 1) * devices)
            gr, gi = g_ref[rows, lanes], g_ref[rows, ilanes]
            y_ref[0, c, rows, :] = gr * tc - gi * ts
            y_ref[1, c, rows, :] = gi * tc + gr * ts
    for c in range(span // LANES):
        def get(part, p):
            return y_ref[part, c, pl.ds(p, fields, stride=devices), :]

        spec = [(get(0, 0), None)]
        for p in range(1, half):
            spec.append(
                ((get(0, p) + get(0, devices - p)) * 0.5, (get(1, p) - get(1, devices - p)) * 0.5)
            )
        spec.append((get(0, half), None))
        for t, value in enumerate(real_idft(spec)):
            write(t, c, value)


def gather_kernel(devices, slots, blocks, nodes, order_ref, mag_ref, out_ref):
    def step(i, carry):
        for b in range(blocks):
            node = order_ref[b * BSIZE + i]
            d, s = i // slots, i % slots
            for c in range(2):
                out_ref[d, s, pl.ds(c * blocks + b, 1), :] = mag_ref[c, pl.ds(node, 1), :]
        return carry

    lax.fori_loop(0, BSIZE, step, 0)


def scatter_kernel(devices, slots, blocks, nodes, order_ref, in_ref, out_ref):
    def step(i, carry):
        for b in range(blocks):
            node = order_ref[b * BSIZE + i]
            d, s = i // slots, i % slots
            for c in range(2):
                out_ref[c, pl.ds(node, 1), :] = in_ref[d, s, pl.ds(c * blocks + b, 1), :]
        return carry

    lax.fori_loop(0, BSIZE, step, 0)


def forward_kernel(devices, slots, fields, recv_ref, wh_ref, wl_ref, tw_ref, b_ref, y_ref, zh_ref, zl_ref):
    for s in range(slots):
        forward_slot(
            lambda t, c: recv_ref[t, s, :, c * LANES : (c + 1) * LANES],
            y_ref, zh_ref, zl_ref, wh_ref, wl_ref, tw_ref, b_ref.at[s], devices, fields,
        )


def back_kernel(devices, slots, blocks, sb_ref, b_ref, zt_ref, wh_ref, wl_ref, tw_ref, out_ref, eh_ref, el_ref, g_ref, y_ref):
    for s in range(slots):
        mix_slot(b_ref.at[s], zt_ref, sb_ref, eh_ref, el_ref, devices, blocks)

        def write(t, c, value):
            out_ref[t, s, :, c * LANES : (c + 1) * LANES] = value

        inverse_slot(eh_ref, el_ref, g_ref, y_ref, wh_ref, wl_ref, tw_ref, write, devices, 2 * blocks)


VM = pl.BlockSpec(memory_space=pltpu.VMEM)
SM = pl.BlockSpec(memory_space=pltpu.SMEM)


def params():
    return pltpu.CompilerParams(vmem_limit_bytes=VMEM_LIMIT)


def local(tables, mag_field, node_order, source_blocks, impedance):
    devices = lax.axis_size("freq")
    nodes = node_order.shape[0]
    blocks = nodes // BSIZE
    slots = BSIZE // devices
    fields = 2 * blocks
    span = NT // devices
    share = impedance.shape[3]
    count = NBR * 8 * blocks
    (fh, fl), (ih, il), twist = tables
    f32, bf16 = jnp.float32, jnp.bfloat16
    rows = fields * devices

    own = impedance.reshape(count, share // LANES, LANES).transpose(1, 0, 2)
    zg = lax.all_gather(own, "freq").reshape(64 * count, LANES)

    laid = pl.pallas_call(
        functools.partial(gather_kernel, devices, slots, blocks, nodes),
        out_shape=jax.ShapeDtypeStruct((devices, slots, fields, span), f32),
        in_specs=[SM, VM], out_specs=VM, compiler_params=params(),
    )(node_order, mag_field)
    recv = lax.all_to_all(laid, "freq", split_axis=0, concat_axis=0, tiled=True)
    zt = pl.pallas_call(
        lambda a, b: turn_impedance(a, b, devices, count),
        out_shape=jax.ShapeDtypeStruct((count, devices, span // 2), f32),
        in_specs=[VM], out_specs=VM, compiler_params=params(),
        cost_estimate=pl.CostEstimate(flops=0, bytes_accessed=16 << 20, transcendentals=0),
    )(zg)
    spectra = pl.pallas_call(
        functools.partial(forward_kernel, devices, slots, fields),
        out_shape=jax.ShapeDtypeStruct((slots, rows, span), f32),
        in_specs=[VM] * 4, out_specs=VM,
        scratch_shapes=[
            pltpu.VMEM((2, span // LANES, rows, LANES), f32),
            pltpu.VMEM((rows, 2 * span), bf16),
            pltpu.VMEM((rows, 2 * span), bf16),
        ],
        compiler_params=params(),
    )(recv, fh, fl, twist)
    series = pl.pallas_call(
        functools.partial(back_kernel, devices, slots, blocks),
        out_shape=jax.ShapeDtypeStruct((devices, slots, fields, span), f32),
        in_specs=[SM] + [VM] * 5, out_specs=VM,
        scratch_shapes=[
            pltpu.VMEM((rows, span), bf16),
            pltpu.VMEM((rows, span), bf16),
            pltpu.VMEM((rows, 2 * span), f32),
            pltpu.VMEM((2, span // LANES, rows, LANES), f32),
        ],
        compiler_params=params(),
    )(source_blocks, spectra, zt, ih, il, twist)
    back = lax.all_to_all(series, "freq", split_axis=0, concat_axis=0, tiled=True)
    return pl.pallas_call(
        functools.partial(scatter_kernel, devices, slots, blocks, nodes),
        out_shape=jax.ShapeDtypeStruct((2, nodes, span), f32),
        in_specs=[SM, VM], out_specs=VM, compiler_params=params(),
    )(node_order, back)


def solution(mesh):
    tables = build_tables(mesh.shape["freq"])
    placed = (
        P(None, "groups", "freq"),
        P("groups"),
        P("groups", None),
        P(None, None, "groups", "freq"),
    )
    return jax.shard_map(
        functools.partial(local, tables),
        mesh=mesh, in_specs=placed, out_specs=P(None, "groups", "freq"), check_vma=False,
    )
```
